32 devices in a mesh: section: 4 (over z), ctx: 2 (over y), head: 4 (over x, core).
Axes of the slice: x: 2, y: 2, z: 4, core: 2. Of those that a mesh axis runs over, the one named last changes fastest.
Arguments:
- first_batch: bfloat16 [4, 512, 8192], P('section', 'ctx', 'head'), may hold values from -6 to 6
- next_batch: bfloat16 [512, 8192], P('ctx', 'head'), may hold values from -6 to 6
- bc_weight: bfloat16 [4, 8192, 256], P('section', 'head'), may hold values from -0.0625 to 0.0625
- dt_weight: bfloat16 [4, 8192, 64], P('section', 'head'), may hold values from -0.0625 to 0.0625
- dt_bias: float32 [4, 64], P('section', 'head'), may hold values from -1 to 1
- decay_rate: float32 [4, 64], P('section', 'head'), may hold values from 0.0003 to 0.05
- skip: float32 [4, 64], P('section', 'head'), may hold values from 0.5 to 1.5
- norm_gain: float32 [4, 8192], P('section', 'head'), may hold values from 0.5 to 1.5
Outputs:
- second_out: bfloat16 [4, 512, 8192], P('section', 'ctx', 'head')
The draws below stay inside these ranges and needn't reach their ends.
All inputs are finite; a program needn't handle non-finite values.
Results may differ from the reference program's by a relative error of at most 0.0095.
Values may be sent and summed in bfloat16 or wider, within the bound.
No kernel may reach another device: no remote copies, remote signals or barrier semaphores. Data moves between devices by JAX's collectives and lax.ppermute only.
A program may use at most 64 MiB of HBM per device.

```python
import math
import jax
import jax.numpy as jnp
from jax import lax

D = 8192
HEADS = 64
N = 128
GROUP = 128
TOKENS = 512
SECTIONS = 4


def block_scale(stream_key, dims, shards, low, top_value):
    level = 1.0
    for position, blocks in shards:
        steps = jax.random.uniform(jax.random.fold_in(jax.random.fold_in(stream_key, 6), position), (blocks,), jnp.float32, low / len(shards), top_value / len(shards))
        level = level * jnp.repeat(jnp.exp(steps), dims[position] // blocks).reshape((-1,) + (1,) * (len(dims) - 1 - position))
    return level


def scatter_about(own_key, dims, scale, most, split=(), kind=jnp.bfloat16):
    result = scale * jax.random.normal(own_key, dims, jnp.float32)
    if split:
        result = result * block_scale(own_key, dims, split, -0.22, 0.18)
    return jnp.clip(result, -most, most).astype(kind)


def setup_inputs(seed: int = 0) -> dict:
    splits = jax.random.split(jax.random.key(seed), 9)
    first_batch = scatter_about(splits[0], (SECTIONS, TOKENS, D), 1.0, 6.0, ((0, 4), (1, 2), (2, 4)))
    next_batch = scatter_about(splits[1], (TOKENS, D), 1.0, 6.0, ((0, 2), (1, 4)))
    bc_weight = scatter_about(splits[2], (SECTIONS, D, 2 * N), D ** -0.5, 0.0625, ((0, 4), (1, 4)))
    dt_weight = scatter_about(splits[3], (SECTIONS, D, HEADS), D ** -0.5, 0.0625, ((0, 4), (1, 4)))
    dt_bias = jnp.clip(jax.random.uniform(splits[4], (SECTIONS, HEADS), jnp.float32, -1.0, 1.0) * block_scale(splits[4], (SECTIONS, HEADS), ((0, 4), (1, 4)), -0.4, 0.0), -1.0, 1.0)
    decay_rate = jnp.clip(jnp.exp(math.log(0.05) - 5.115996 * jax.random.uniform(splits[5], (SECTIONS, HEADS), jnp.float32) ** block_scale(splits[5], (SECTIONS, HEADS), ((0, 4), (1, 4)), -0.2, 0.2)), 0.0003, 0.05)
    skip = jnp.clip(0.5 + 1.0 * jax.random.uniform(splits[6], (SECTIONS, HEADS), jnp.float32) ** block_scale(splits[6], (SECTIONS, HEADS), ((0, 4), (1, 4)), -0.2, 0.2), 0.5, 1.5)
    norm_gain = jnp.clip(1.0 + 0.1 * jax.random.normal(splits[7], (SECTIONS, D), jnp.float32), 0.5, 1.5)
    return dict(first_batch=first_batch, next_batch=next_batch, bc_weight=bc_weight, dt_weight=dt_weight, dt_bias=dt_bias, decay_rate=decay_rate, skip=skip, norm_gain=norm_gain)


def block_step(state, x_blk, b_blk, c_blk, dt_blk, rate):
    logs = -dt_blk * rate[None, :]
    cum = jnp.cumsum(logs, axis=0)
    cum_t = cum.T
    size = x_blk.shape[0]
    rows = lax.broadcasted_iota(jnp.int32, (size, size), 0)
    cols = lax.broadcasted_iota(jnp.int32, (size, size), 1)
    causal = rows >= cols
    scores = jnp.dot(c_blk, b_blk.T, preferred_element_type=jnp.float32)
    diff = cum_t[:, :, None] - cum_t[:, None, :]
    decay = jnp.exp(jnp.where(causal[None], diff, 0.0)) * dt_blk.T[:, None, :]
    weights = jnp.where(causal[None], decay * scores[None], 0.0).astype(jnp.bfloat16)
    y_blk = jnp.einsum('hts,shp->thp', weights.astype(jnp.float32), x_blk.astype(jnp.float32), precision=lax.Precision.HIGHEST)
    end = cum[-1]
    scaled_b = (b_blk.astype(jnp.float32)[:, None, :] * (jnp.exp(end[None, :] - cum) * dt_blk)[:, :, None]).astype(jnp.bfloat16)
    contrib = jnp.einsum('shn,shp->hnp', scaled_b.astype(jnp.float32), x_blk.astype(jnp.float32), precision=lax.Precision.HIGHEST)
    inter = jnp.einsum('tn,hnp->thp', c_blk.astype(jnp.float32), state, precision=lax.Precision.HIGHEST)
    y_blk = y_blk + inter * jnp.exp(cum)[:, :, None]
    new_state = jnp.exp(end)[:, None, None] * state + contrib
    return (new_state, y_blk)

def mixer(x, w_bc, w_dt, bias, rate, skip, gain):
    tokens, width = x.shape
    heads = w_dt.shape[1]
    hdim = width // heads
    nstate = w_bc.shape[1] // 2
    proj = jnp.dot(x, w_bc, preferred_element_type=jnp.float32)
    b_mat = proj[:, :nstate].astype(jnp.bfloat16)
    c_mat = proj[:, nstate:].astype(jnp.bfloat16)
    steps = jax.nn.softplus(jnp.dot(x, w_dt, preferred_element_type=jnp.float32) + bias[None, :])
    blocks = tokens // GROUP
    x_heads = x.reshape(blocks, GROUP, heads, hdim)
    b_blocks = b_mat.reshape(blocks, GROUP, nstate)
    c_blocks = c_mat.reshape(blocks, GROUP, nstate)
    dt_blocks = steps.reshape(blocks, GROUP, heads)

    def advance(state, pieces):
        return block_step(state, pieces[0], pieces[1], pieces[2], pieces[3], rate)
    start = jnp.zeros((heads, nstate, hdim), jnp.float32)
    final, ys = lax.scan(advance, start, (x_heads, b_blocks, c_blocks, dt_blocks))
    y_all = ys.reshape(tokens, heads, hdim) + skip[None, :, None] * x.reshape(tokens, heads, hdim).astype(jnp.float32)
    meansq = lax.optimization_barrier(jnp.mean(y_all * y_all, axis=(1, 2)))
    normed = (y_all * lax.rsqrt(meansq + 1e-05)[:, None, None]).reshape(tokens, width) * gain[None, :]
    return (x.astype(jnp.float32) + normed).astype(jnp.bfloat16)

def reference(first_batch, next_batch, bc_weight, dt_weight, dt_bias, decay_rate, skip, norm_gain):

    def one_layer(items):
        return mixer(items[0], items[1], items[2], items[3], items[4], items[5], items[6])
    first_out = lax.map(one_layer, (first_batch, bc_weight, dt_weight, dt_bias, decay_rate, skip, norm_gain))
    entry = jnp.concatenate([next_batch[None], first_out[:-1]], axis=0)
    second_out = lax.map(one_layer, (entry, bc_weight, dt_weight, dt_bias, decay_rate, skip, norm_gain))
    return second_out
```

```python
import functools
import math

import jax
import jax.numpy as jnp
from jax import lax
from jax.experimental import pallas as pl
from jax.experimental.pallas import tpu as pltpu
from jax.sharding import PartitionSpec as P

GROUP = 128
LANES = 128
F32 = jnp.float32
BF16 = jnp.bfloat16
LOG2E = math.log2(math.e)
EPS = 1e-05
PARAMS = pltpu.CompilerParams(vmem_limit_bytes=24 * 2**20)
SMEM = pl.BlockSpec(memory_space=pltpu.SMEM)


def vmem(count):
    return [pl.BlockSpec(memory_space=pltpu.VMEM)] * count


def shape(dims, kind):
    return jax.ShapeDtypeStruct(dims, kind)


def dot(a, b):
    return jnp.dot(a, b, preferred_element_type=F32)


def partner(i, k, count):
    return i ^ k if count & (count - 1) == 0 else (i + k) % count


def hop(block, axis, k):
    count = lax.axis_size(axis)
    return lax.ppermute(block, axis, [(i, partner(i, k, count)) for i in range(count)])


def onward(block):
    count = lax.axis_size("section")
    return lax.ppermute(block, "section", [(i, (i + 1) % count) for i in range(count)])


def project(x, wbc_ref, wdt_ref, flags, steps_ref, own_b, own_c, own_dt, packs):
    tokens = x.shape[0]
    heads = own_dt.shape[0]
    nstate = own_b.shape[1]
    bc = dot(x, wbc_ref[...])
    own_b[...] = bc[:, :nstate]
    own_c[...] = bc[:, nstate:]
    steps_ref[...] = dot(x, wdt_ref[...]).T
    me = flags[0]
    own_dt[...] = steps_ref[pl.ds(pl.multiple_of(me * heads, heads), heads), :]
    count = len(packs) + 1
    for k, pack in enumerate(packs, 1):
        pack[:tokens, :] = bc[:, :nstate]
        at = partner(me, k, count) * heads
        part = steps_ref[pl.ds(pl.multiple_of(at, heads), heads), :]
        for i in range(tokens // LANES):
            pack[tokens + i * heads : tokens + (i + 1) * heads, :] = part[:, i * LANES : (i + 1) * LANES]


def head_sum(own_b, own_dt, packs, bias, rate):
    tokens = own_b.shape[0]
    heads = own_dt.shape[0]
    b_mat = own_b[...]
    pre = own_dt[...]
    for pack in packs:
        b_mat = b_mat + pack[:tokens, :]
        pre = pre + jnp.concatenate(
            [pack[tokens + i * heads : tokens + (i + 1) * heads, :] for i in range(tokens // LANES)], axis=1
        )
    pre = pre + bias
    dt = jnp.maximum(pre, 0.0) + jnp.log1p(jnp.exp(-jnp.abs(pre)))
    logs = dt * (rate * -LOG2E)
    high = logs.astype(BF16)
    rest = logs - high.astype(F32)
    mid = rest.astype(BF16)
    low = (rest - mid.astype(F32)).astype(BF16)
    row = lax.broadcasted_iota(jnp.int32, (tokens, tokens), 0)
    col = lax.broadcasted_iota(jnp.int32, (tokens, tokens), 1)
    upto = (row <= col).astype(F32).astype(BF16)
    cum = (dot(high, upto) + dot(mid, upto)) + dot(low, upto)
    return b_mat.astype(BF16), dt, cum


def states(b_mat, dt, cum, x, first, out):
    tokens = b_mat.shape[0]
    b_t = b_mat.astype(F32).T
    scale = jnp.exp2(cum[:, tokens - 1 : tokens] - cum) * dt
    for j in range(out.shape[0]):
        h = first + j
        scaled = (b_t * scale[h : h + 1, :]).astype(BF16)
        out[j] = dot(scaled, x[:, j * LANES : (j + 1) * LANES]).astype(BF16)


def columns(cum):
    heads, tokens = cum.shape
    return jnp.concatenate([cum, jnp.zeros((LANES - heads, tokens), F32)], axis=0).T


def inner(b_mat, c_mat, dt, cum, skip_rows, x, first, y):
    tokens = b_mat.shape[0]
    scores = lax.dot_general(c_mat, b_mat, (((1,), (1,)), ((), ())), preferred_element_type=F32)
    row = lax.broadcasted_iota(jnp.int32, (tokens, tokens), 0)
    col = lax.broadcasted_iota(jnp.int32, (tokens, tokens), 1)
    scores = jnp.where(row >= col, scores, 0.0)
    cum_c = columns(cum)
    for j in range(y.shape[1] // LANES):
        h = first + j
        at = slice(j * LANES, (j + 1) * LANES)
        x_h = x[:, at]
        skip = skip_rows[h // 2 : h // 2 + 1, (h % 2) * LANES : (h % 2 + 1) * LANES]
        for i in range(tokens // GROUP):
            rows = slice(i * GROUP, (i + 1) * GROUP)
            upto = (i + 1) * GROUP
            diff = jnp.minimum(cum_c[rows, h : h + 1] - cum[h : h + 1, :upto], 0.0)
            weights = (jnp.exp2(diff) * scores[rows, :upto] * dt[h : h + 1, :upto]).astype(BF16)
            y[rows, at] = dot(weights, x_h[:upto, :]) + skip * x_h[rows, :].astype(F32)


def carried(c_mat, cum, prior, y_in, first, keep, y_out):
    tokens = c_mat.shape[0]
    cum_c = jnp.exp2(columns(cum)) * keep
    squares = jnp.zeros((tokens, LANES), F32)
    for j in range(prior.shape[0]):
        h = first + j
        at = slice(j * LANES, (j + 1) * LANES)
        y = y_in[:, at] + dot(c_mat, prior[j]) * cum_c[:, h : h + 1]
        y_out[:, at] = y
        squares = squares + y * y
    return jnp.sum(squares.T.reshape(LANES // 8, 8, tokens), axis=0)


def norm_scale(sums, width):
    total = sums[0][...]
    for s in sums[1:]:
        total = total + s[...]
    row = lax.rsqrt(jnp.sum(total, axis=0, keepdims=True) / width + EPS)
    return jnp.broadcast_to(row, (LANES, row.shape[1])).T


def gain_of(aux, base, h):
    return aux[base + h // 2 : base + h // 2 + 1, (h % 2) * LANES : (h % 2 + 1) * LANES]


def first_kernel(peers, flags, x, wbc, wdt, own_b, own_c, own_dt, *rest):
    project(x[...], wbc, wdt, flags, rest[peers], own_b, own_c, own_dt, rest[:peers])


def sum_kernel(peers, own_b, own_dt, *rest):
    packs = rest[:peers]
    bias, rate, skip, gain, b_out, aux = rest[peers:]
    heads = own_dt.shape[0]
    b_mat, dt, cum = head_sum(own_b, own_dt, packs, bias[...], rate[...])
    b_out[...] = b_mat
    aux[:heads, :] = dt
    aux[heads : 2 * heads, :] = cum
    for i in range(heads // 2):
        at = slice(2 * i * LANES, 2 * (i + 1) * LANES)
        aux[2 * heads + i : 2 * heads + i + 1, :] = skip[:, at]
        aux[2 * heads + heads // 2 + i : 2 * heads + heads // 2 + i + 1, :] = gain[:, at]


def add_kernel(*refs):
    total = refs[0][...]
    for ref in refs[1:-1]:
        total = total + ref[...]
    refs[-1][...] = total.astype(refs[-1].dtype)


def state_kernel(first, heads, b_mat, aux, x, out):
    states(b_mat[...], aux[:heads, :], aux[heads : 2 * heads, :], x, first, out)


def inner_kernel(first, heads, b_mat, c_mat, aux, x, y):
    skip_rows = aux[2 * heads : 2 * heads + heads // 2, :]
    inner(b_mat[...], c_mat[...], aux[:heads, :], aux[heads : 2 * heads, :], skip_rows, x, first, y)


def carry_kernel(first, heads, before, flags, c_mat, aux, prior, y_in, *rest):
    y_out, squares = rest[before:]
    keep = jnp.where(flags[2] > 0, 1.0, 0.0)
    own = carried(c_mat[...], aux[heads : 2 * heads, :], prior, y_in, first, keep, y_out)
    squares[...] = own + rest[0][...] if before else own


def entry_kernel(peers, chunks, heads, width, flags, aux, fresh, wbc, wdt, *rest):
    sums, rest = rest[: peers + 1], rest[peers + 1 :]
    xs, ys, rest = rest[:chunks], rest[chunks : 2 * chunks], rest[2 * chunks :]
    entry, own_b, own_c, own_dt = rest[:4]
    packs, steps = rest[4 : 4 + peers], rest[4 + peers]
    scale = norm_scale(sums, width)
    h = 0
    for x, y in zip(xs, ys):
        for j in range(x.shape[1] // LANES):
            at = slice(j * LANES, (j + 1) * LANES)
            to = slice(h * LANES, (h + 1) * LANES)
            gain = gain_of(aux, 2 * heads + heads // 2, h)
            made = (x[:, at].astype(F32) + y[:, at] * scale * gain).astype(BF16)
            entry[:, to] = jnp.where(flags[1] > 0, made, fresh[:, to])
            h += 1
    project(entry[...], wbc, wdt, flags, steps, own_b, own_c, own_dt, packs)


def out_kernel(peers, chunks, heads, width, aux, entry, *rest):
    sums, ys, out = rest[: peers + 1], rest[peers + 1 : -1], rest[-1]
    scale = norm_scale(sums, width)
    h = 0
    for y in ys:
        for j in range(y.shape[1] // LANES):
            at = slice(j * LANES, (j + 1) * LANES)
            to = slice(h * LANES, (h + 1) * LANES)
            gain = gain_of(aux, 2 * heads + heads // 2, h)
            out[:, to] = (entry[:, to].astype(F32) + y[:, at] * scale * gain).astype(BF16)
            h += 1


def earlier_state(own, total):
    count, mine = lax.axis_size("ctx"), lax.axis_index("ctx")
    if count == 2:
        return hop(own, "ctx", 1)
    all_states = lax.all_gather(own, "ctx").astype(F32)
    ends = lax.all_gather(total, "ctx")
    prior = jnp.zeros(own.shape, F32)
    for k in range(count):
        later = jnp.exp2(ends[k])[:, None, None] * prior + all_states[k]
        prior = jnp.where(k < mine, later, prior)
    return prior.astype(BF16)


def all_sums(own):
    return [own] + [hop(own, "head", k) for k in range(1, lax.axis_size("head"))]


def shards(first_batch, next_batch, bc_weight, dt_weight, dt_bias, decay_rate, skip, norm_gain):
    x_first, wbc, wdt = first_batch[0], bc_weight[0], dt_weight[0]
    tokens, width = x_first.shape
    heads = dt_bias.shape[1]
    nstate = wbc.shape[1] // 2
    peers = lax.axis_size("head") - 1
    all_width = width * (peers + 1)
    flags = jnp.stack(
        [lax.axis_index("head"), lax.axis_index("section"), lax.axis_index("ctx"), 0]
    ).astype(jnp.int32)
    bias = dt_bias.T
    rate = decay_rate.T
    skip_row = jnp.repeat(skip, width // heads, axis=1)

    proj_out = (
        [shape((tokens, nstate), F32)] * 2
        + [shape((heads, tokens), F32)]
        + [shape((tokens + heads * (tokens // LANES), nstate), F32)] * peers
    )
    proj_scratch = [pltpu.VMEM((wdt.shape[1], tokens), F32)]
    mat_shape = shape((tokens, nstate), BF16)
    aux_shape = shape((3 * heads, tokens), F32)

    def sum_over_head(own_b, own_c, own_dt, packs):
        packs = [hop(p, "head", k) for k, p in enumerate(packs, 1)]
        parts = [own_c] + [hop(own_c, "head", k) for k in range(1, peers + 1)]
        b_mat, aux = pl.pallas_call(
            functools.partial(sum_kernel, peers),
            out_shape=[mat_shape, aux_shape],
            in_specs=vmem(6 + peers),
            out_specs=vmem(2),
            compiler_params=PARAMS,
            name="sum_b",
        )(own_b, own_dt, *packs, bias, rate, skip_row, norm_gain)
        c_mat = pl.pallas_call(
            add_kernel,
            out_shape=mat_shape,
            in_specs=vmem(1 + peers),
            out_specs=vmem(1)[0],
            compiler_params=PARAMS,
            name="sum_c",
        )(*parts)
        return b_mat, c_mat, aux

    def scan(b_mat, c_mat, aux, xs, sizes):
        ys, priors, firsts = [], [], []
        first = 0
        totals = aux[heads : 2 * heads, -1]
        for x, size in zip(xs, sizes):
            own = pl.pallas_call(
                functools.partial(state_kernel, first, heads),
                out_shape=shape((size, nstate, LANES), BF16),
                in_specs=vmem(3),
                out_specs=vmem(1)[0],
                compiler_params=PARAMS,
                name="states",
            )(b_mat, aux, x)
            priors.append(earlier_state(own, totals[first : first + size]))
            firsts.append(first)
            first += size
        for x, size, first in zip(xs, sizes, firsts):
            ys.append(
                pl.pallas_call(
                    functools.partial(inner_kernel, first, heads),
                    out_shape=shape((tokens, size * LANES), F32),
                    in_specs=vmem(4),
                    out_specs=vmem(1)[0],
                    compiler_params=PARAMS,
                    name="inner",
                )(b_mat, c_mat, aux, x)
            )
        squares = []
        for i, size in enumerate(sizes):
            ys[i], made = pl.pallas_call(
                functools.partial(carry_kernel, firsts[i], heads, len(squares)),
                out_shape=[shape((tokens, size * LANES), F32), shape((8, tokens), F32)],
                in_specs=[SMEM] + vmem(4 + len(squares)),
                out_specs=vmem(2),
                compiler_params=PARAMS,
                name="carry",
            )(flags, c_mat, aux, priors[i], ys[i], *squares)
            squares = [made]
        return ys, all_sums(squares[0])

    sizes = [heads // 2, heads // 4, heads - heads // 2 - heads // 4]
    edges = [0, sizes[0], sizes[0] + sizes[1], heads]
    cuts = [x_first[:, a * LANES : b * LANES] for a, b in zip(edges, edges[1:])]
    moved = [onward(cuts[0])]
    own_b, own_c, own_dt, *packs = pl.pallas_call(
        functools.partial(first_kernel, peers),
        out_shape=proj_out,
        in_specs=[SMEM] + vmem(3),
        out_specs=vmem(3 + peers),
        scratch_shapes=proj_scratch,
        compiler_params=PARAMS,
        name="project",
    )(flags, x_first, wbc, wdt)
    b_mat, c_mat, aux = sum_over_head(own_b, own_c, own_dt, packs)
    b_mat, aux, *rest = lax.optimization_barrier((b_mat, aux, *cuts[1:]))
    b_mat, aux = onward(b_mat), onward(aux)
    moved.append(onward(rest[0]))
    c_mat, last = lax.optimization_barrier((c_mat, rest[1]))
    c_mat = onward(c_mat)
    moved.append(onward(last))
    ys, sums = scan(b_mat, c_mat, aux, moved, sizes)

    entry, own_b, own_c, own_dt, *packs = pl.pallas_call(
        functools.partial(entry_kernel, peers, len(sizes), heads, all_width),
        out_shape=[shape((tokens, width), BF16)] + proj_out,
        in_specs=[SMEM] + vmem(5 + peers + 2 * len(sizes)),
        out_specs=vmem(4 + peers),
        scratch_shapes=proj_scratch,
        compiler_params=PARAMS,
        name="entry",
    )(flags, aux, next_batch, wbc, wdt, *sums, *moved, *ys)

    b_mat, c_mat, aux = sum_over_head(own_b, own_c, own_dt, packs)
    ys, sums = scan(b_mat, c_mat, aux, [entry], [heads])
    out = pl.pallas_call(
        functools.partial(out_kernel, peers, 1, heads, all_width),
        out_shape=shape((tokens, width), BF16),
        in_specs=vmem(3 + peers + 1),
        out_specs=vmem(1)[0],
        compiler_params=PARAMS,
        name="finish",
    )(aux, entry, *sums, *ys)
    return out[None]


def solution(mesh):
    placed = (
        P("section", "ctx", "head"),
        P("ctx", "head"),
        P("section", "head", None),
        P("section", "head", None),
        P("section", "head"),
        P("section", "head"),
        P("section", "head"),
        P("section", "head"),
    )
    return jax.shard_map(
        shards, mesh=mesh, in_specs=placed, out_specs=P("section", "ctx", "head"), check_vma=False
    )
```
